32 devices in a mesh: group: 4 (over z), sub: 8 (over y, x, core).
Axes of the slice: x: 2, y: 2, z: 4, core: 2. Of those that a mesh axis runs over, the one named last changes fastest.
Arguments:
- coords: float32 [3, 131072], P(None, ('group', 'sub')), may hold values from 0 to 1
- charges: bfloat16 [16, 131072], P(None, ('group', 'sub')), may hold values from -6 to 6
- leaf_basis: bfloat16 [1024, 64, 128], P(('group', 'sub')), may hold values from -0.5 to 0.5
- transfer: bfloat16 [1024, 64, 64], P(('group', 'sub')), may hold values from -0.25 to 0.25
- leaf_skeleton: float32 [3, 65536], P(None, ('group', 'sub')), may hold values from 0 to 1
- parent_skeleton: float32 [3, 8192], P(None, ('group', 'sub')), may hold values from 0 to 1
- near_ids: int32 [1024, 27], P(('group', 'sub')), may hold values from 0 to 1023, as said below
- near_mask: int32 [1024, 27], P(('group', 'sub')), may hold values 0 or 1
- far_ids: int32 [1024, 64], P(('group', 'sub')), may hold values from 0 to 1023, as said below
- far_mask: int32 [1024, 64], P(('group', 'sub')), may hold values 0 or 1
- coarse_ids: int32 [128, 64], P(('group', 'sub')), may hold values from 0 to 127
- coarse_mask: int32 [128, 64], P(('group', 'sub')), may hold values 0 or 1
Outputs:
- product: float32 [16, 131072], P(None, ('group', 'sub'))
The draws below stay inside these ranges and needn't reach their ends.
Inputs may be any that keep to these rules, and one draw needn't show every extreme that they name: `near_ids`: entry n of leaf i names a leaf of i's group of 256 leaves at most 32 leaves away from i in leaf order; entry 0 names i itself. `far_ids`: every entry names a leaf of the same group of 256 leaves.
All inputs are finite; a program needn't handle non-finite values. No bound on the sum of `near_mask` or of `far_mask` or of `coarse_mask` on one device may be relied on, other than what follows from the above.
Results may differ from the reference program's by a relative error of at most 0.014.
Values may be sent and summed in bfloat16 or wider, within the bound.
A program may use at most 128 MiB of HBM per device.

```python
import math
import jax
import jax.numpy as jnp
from jax import lax

LD = 32
P_SIZE = 128
K = 64
R = 16
CH = 8
NEAR = 27
FAR = 64
CFAR = 64
LEAVES = 1024
PARENTS = 128
GROUP_LEAVES = 256
NPTS = 131072


def draw_near_ids(key, part):
    key = jax.random.fold_in(key, 11)
    leaf_index = jnp.arange(LEAVES, dtype=jnp.int32)[:, None]
    moves = jax.random.randint(key, (LEAVES, NEAR), -LD, LD + 1, dtype=jnp.int32)
    group_start = leaf_index // GROUP_LEAVES * GROUP_LEAVES
    chosen = jnp.clip(leaf_index + moves, group_start, group_start + GROUP_LEAVES - 1)
    column = jnp.arange(NEAR, dtype=jnp.int32)[None, :]
    return jnp.where(column == 0, leaf_index, chosen).astype(jnp.int32)


def draw_far_ids(key, part):
    key = jax.random.fold_in(key, 23)
    leaf_index = jnp.arange(LEAVES, dtype=jnp.int32)[:, None]
    group_start = leaf_index // GROUP_LEAVES * GROUP_LEAVES
    picked = jax.random.randint(key, (LEAVES, FAR), 0, GROUP_LEAVES, dtype=jnp.int32)
    return (group_start + picked).astype(jnp.int32)


def with_ends(result, own_key, least, largest):
    dims = result.shape
    spot = [jax.random.randint(jax.random.fold_in(own_key, axis), (), 0, dims[axis]) for axis in range(len(dims))]
    result = result.at[tuple(spot)].set(least)
    longest = dims.index(max(dims))
    spot[longest] = (spot[longest] + 1) % dims[longest]
    return result.at[tuple(spot)].set(largest)


def shard_levels(key, dims, shards, low, largest):
    def one(position, parts):
        steps = jax.random.uniform(jax.random.fold_in(jax.random.fold_in(key, 6), position), (parts,), jnp.float32, low / len(shards), largest / len(shards))
        return jnp.repeat(jnp.exp(steps), dims[position] // parts).reshape((-1,) + (1,) * (len(dims) - position - 1))

    level = one(*shards[0])
    for cut in shards[1:]:
        level = level * one(*cut)
    return level


def scatter_about(stream_key, shape, scale, reach, cuts=(), kind=jnp.bfloat16):
    drawn = jax.random.normal(stream_key, shape, jnp.float32) * scale
    if len(cuts) > 0:
        drawn = shard_levels(stream_key, shape, cuts, -0.22, 0.18) * drawn
    return jnp.clip(drawn, min=-reach, max=reach).astype(kind)


def setup_inputs(seed: int = 0) -> dict:
    arg_keys = jax.random.split(jax.random.key(seed), 13)
    return {
        "coords": jnp.clip(1.0 * jax.random.uniform(arg_keys[0], (3, NPTS), jnp.float32) ** shard_levels(arg_keys[0], (3, NPTS), ((1, 32),), -0.2, 0.2), 0.0, 1.0),
        "charges": scatter_about(arg_keys[1], (R, NPTS), 1.0, 6.0, ((1, 32),)),
        "leaf_basis": scatter_about(arg_keys[2], (LEAVES, K, P_SIZE), P_SIZE ** -0.5, 0.5, ((0, 32),)),
        "transfer": scatter_about(arg_keys[3], (LEAVES, K, K), (CH * K) ** -0.5, 0.25, ((0, 32),)),
        "leaf_skeleton": jnp.clip(1.0 * jax.random.uniform(arg_keys[4], (3, LEAVES * K), jnp.float32) ** shard_levels(arg_keys[4], (3, LEAVES * K), ((1, 32),), -0.2, 0.2), 0.0, 1.0),
        "parent_skeleton": jnp.clip(1.0 * jax.random.uniform(arg_keys[5], (3, PARENTS * K), jnp.float32) ** shard_levels(arg_keys[5], (3, PARENTS * K), ((1, 32),), -0.2, 0.2), 0.0, 1.0),
        "near_ids": draw_near_ids(jax.random.fold_in(arg_keys[12], 71), 0),
        "near_mask": with_ends((jax.random.randint(arg_keys[7], (LEAVES, NEAR), 0, 5) < 4).astype(jnp.int32), jax.random.fold_in(arg_keys[7], 1), 0, 1),
        "far_ids": draw_far_ids(jax.random.fold_in(arg_keys[12], 71), 0),
        "far_mask": with_ends((jax.random.randint(arg_keys[9], (LEAVES, FAR), 0, 5) < 4).astype(jnp.int32), jax.random.fold_in(arg_keys[9], 1), 0, 1),
        "coarse_ids": with_ends(jax.random.randint(arg_keys[10], (PARENTS, CFAR), 0, PARENTS), jax.random.fold_in(arg_keys[10], 1), 0, PARENTS - 1).astype(jnp.int32),
        "coarse_mask": with_ends((jax.random.randint(arg_keys[11], (PARENTS, CFAR), 0, 5) < 4).astype(jnp.int32), jax.random.fold_in(arg_keys[11], 1), 0, 1),
    }


root_three = 1.7320508075688772
length_scale = 0.25

def matern(targets, sources):
    spread = targets[..., :, None] - sources[..., None, :]
    radius = jnp.sqrt(lax.optimization_barrier(jnp.sum(spread * spread, axis=0)))
    scaled = root_three / length_scale * radius
    return (1.0 + scaled) * jnp.exp(-scaled)

def masked_tile(targets, sources, valid):
    values = matern(targets[:, :, None, :], sources)
    return (values * valid[:, :, None, None].astype(jnp.float32)).astype(jnp.bfloat16)

def list_product(targets, sources, source_values, valid, factor):
    kernel_tile = masked_tile(targets, sources, valid)
    summed = jnp.einsum('bfts,rbfs->rbt', kernel_tile.astype(jnp.float32), source_values.astype(jnp.float32))
    return summed * factor

def blocked(block_rows, target_points, list_ids, list_valid, source_points, source_values, factor):
    total_rows = target_points.shape[1]

    def one_block(block_index):
        first_row = block_index * block_rows
        chosen = lax.dynamic_slice_in_dim(list_ids, first_row, block_rows, 0)
        valid = lax.dynamic_slice_in_dim(list_valid, first_row, block_rows, 0)
        targets = lax.dynamic_slice_in_dim(target_points, first_row, block_rows, 1)
        sources = jnp.take(source_points, chosen, axis=1)
        values = jnp.take(source_values, chosen, axis=1)
        return list_product(targets, sources, values, valid, factor)
    pieces = lax.map(one_block, jnp.arange(total_rows // block_rows, dtype=jnp.int32))
    return jnp.moveaxis(pieces, 0, 1).reshape(source_values.shape[0], total_rows, -1)

def reference(coords, charges, leaf_basis, transfer, leaf_skeleton, parent_skeleton, near_ids, near_mask, far_ids, far_mask, coarse_ids, coarse_mask):
    leaf_count = leaf_basis.shape[0]
    parent_count = leaf_count // CH
    points = coords.reshape(3, leaf_count, P_SIZE)
    leaf_charges = charges.reshape(R, leaf_count, P_SIZE)
    leaf_coefs = jnp.einsum('rlp,lkp->rlk', leaf_charges.astype(jnp.float32), leaf_basis.astype(jnp.float32)).astype(jnp.bfloat16)
    child_maps = transfer.reshape(parent_count, CH, K, K).astype(jnp.float32)
    parent_coefs = jnp.einsum('bckj,rbcj->rbk', child_maps, leaf_coefs.reshape(R, parent_count, CH, K).astype(jnp.float32)).astype(jnp.bfloat16)
    near_part = blocked(8, points, near_ids, near_mask, points, leaf_charges, 1.0 / math.sqrt(NEAR))
    skeleton_points = leaf_skeleton.reshape(3, leaf_count, K)
    far_local = blocked(8, skeleton_points, far_ids, far_mask, skeleton_points, leaf_coefs, 1.0 / math.sqrt(FAR))
    parent_points = parent_skeleton.reshape(3, parent_count, K)
    coarse_local = blocked(8, parent_points, coarse_ids, coarse_mask, parent_points, parent_coefs, 1.0 / math.sqrt(CFAR)).astype(jnp.bfloat16)
    downward = jnp.einsum('bckj,rbk->rbcj', child_maps, coarse_local.astype(jnp.float32)).reshape(R, leaf_count, K)
    combined = (far_local + downward).astype(jnp.bfloat16)
    far_out = jnp.einsum('rlk,lkp->rlp', combined.astype(jnp.float32), leaf_basis.astype(jnp.float32))
    return (near_part + far_out).reshape(R, leaf_count * P_SIZE)
```

```python
import functools
import math

import jax
import jax.numpy as jnp
from jax import lax
from jax.experimental import pallas as pl
from jax.experimental.pallas import tpu as pltpu
from jax.sharding import PartitionSpec as P

CH = 8
SHIFT = 64
UNROLL_NEAR = 4
UNROLL_FAR = 8
LOG2E = 1.4426950408889634
STRETCH = math.sqrt(3.0) / 0.25 * LOG2E


def split_points(points):
    scaled = (points - 0.5) * STRETCH
    high = lax.reduce_precision(scaled, 8, 7)
    low = lax.reduce_precision(scaled - high, 8, 7)
    whole = high + low
    norm = jnp.sum(whole * whole, axis=0, keepdims=True)
    n1 = lax.reduce_precision(norm, 8, 7)
    n2 = lax.reduce_precision(norm - n1, 8, 7)
    n3 = norm - n1 - n2
    return high, low, jnp.concatenate([n1, n2, n3], axis=0)


def source_rows(points):
    high, low, norm = split_points(points)
    ones = jnp.ones_like(high)
    return jnp.concatenate([high, high, low, ones, norm, jnp.zeros_like(high[:1])], axis=0).astype(
        jnp.bfloat16
    )


def target_rows(points):
    high, low, norm = split_points(points)
    ones = jnp.ones_like(high)
    return jnp.concatenate(
        [-2.0 * high, -2.0 * low, -2.0 * high, norm, ones, jnp.zeros_like(high[:1])], axis=0
    ).astype(jnp.bfloat16)


def compact(ids, mask):
    slots = ids.shape[1]
    valid = mask != 0
    same = (ids[:, :, None] == ids[:, None, :]) & valid[:, None, :]
    earlier = jnp.arange(slots)[None, :, None] > jnp.arange(slots)[None, None, :]
    count = jnp.sum(same.astype(jnp.int32), axis=2)
    repeated = jnp.any(same & earlier, axis=2)
    first = (valid & ~repeated).astype(jnp.int32)
    place = jnp.sum(jnp.where(earlier, first[:, None, :], 0), axis=2)
    packed = (ids * (2 * SHIFT) + count) * first
    hit = place[:, None, :] == jnp.arange(slots)[None, :, None]
    out = jnp.sum(jnp.where(hit, packed[:, None, :], 0), axis=2)
    return out, jnp.sum(first, axis=1)


def work_items(lengths, per_item, slots, unroll):
    rows = lengths.shape[0]
    items = (lengths + per_item - 1) // per_item
    row = jnp.arange(rows)
    ends = jnp.sum(jnp.where(row[None, :] <= row[:, None], items[None, :], 0), axis=1)
    starts = ends - items
    total = jnp.sum(items)
    most = rows * (-(-slots // per_item))
    most = -(-most // unroll) * unroll
    place = jnp.arange(most)
    owner = jnp.sum((place[:, None] >= ends[None, :]).astype(jnp.int32), axis=1)
    mine = owner[:, None] == row[None, :]
    step = place - jnp.sum(jnp.where(mine, starts[None, :], 0), axis=1)
    entry = jnp.where(owner < rows, owner * slots + step * per_item, rows * slots)
    owner = jnp.minimum(owner, rows - 1)
    trips = (total + unroll - 1) // unroll
    return owner.astype(jnp.int32), entry.astype(jnp.int32), trips.reshape(1).astype(jnp.int32)


def tile_values(squared):
    squared = jnp.maximum(squared, 1e-12)
    u = squared * lax.rsqrt(squared)
    return ((u + LOG2E) * jnp.exp2(-u)).astype(jnp.bfloat16)


def entry_parts(word):
    return word // (2 * SHIFT), (word % (2 * SHIFT)).astype(jnp.float32)


def near_kernel(factor, trips, owner, entry, words, targets, sources, out):
    out[...] = jnp.zeros_like(out)

    def step(i, carry):
        for k in range(UNROLL_NEAR):
            item = i * UNROLL_NEAR + k
            leaf, first = owner[item], entry[item]
            ia, ca = entry_parts(words[first])
            ib, cb = entry_parts(words[first + 1])
            points = jnp.concatenate([sources[ia, :16, :], sources[ib, :16, :]], axis=1)
            va = (sources[ia, 16:, :].astype(jnp.float32) * ca).astype(jnp.bfloat16)
            vb = (sources[ib, 16:, :].astype(jnp.float32) * cb).astype(jnp.bfloat16)
            values = jnp.concatenate([va, vb], axis=1)
            squared = jnp.dot(targets[leaf], points, preferred_element_type=jnp.float32)
            tile = tile_values(squared)
            out[leaf] += factor * lax.dot_general(
                values, tile, (((1,), (1,)), ((), ())), preferred_element_type=jnp.float32
            )
        return carry

    lax.fori_loop(0, trips[0], step, 0)


def far_items(factor, trips, owner, entry, words, targets, spread, total):
    left = lax.broadcasted_iota(jnp.int32, (16, 128), 1) < 64

    def step(i, carry):
        for k in range(UNROLL_FAR):
            item = i * UNROLL_FAR + k
            row, first = owner[item], entry[item]
            points, values = [], []
            for h in range(2):
                ia, ca = entry_parts(words[first + 2 * h])
                ib, cb = entry_parts(words[first + 2 * h + 1])
                points.append(jnp.where(left, spread[ia, :16, :], spread[ib, :16, :]))
                both = jnp.where(
                    left,
                    spread[ia, 16:, :].astype(jnp.float32) * ca,
                    spread[ib, 16:, :].astype(jnp.float32) * cb,
                )
                values.append(both.astype(jnp.bfloat16))
            squared = jnp.dot(
                targets[row], jnp.concatenate(points, axis=1), preferred_element_type=jnp.float32
            )
            tile = tile_values(squared)
            total[row] += factor * lax.dot_general(
                jnp.concatenate(values, axis=1),
                tile,
                (((1,), (1,)), ((), ())),
                preferred_element_type=jnp.float32,
            )
        return carry

    lax.fori_loop(0, trips[0], step, 0)


def spread_halves(packed, spread):
    left = lax.broadcasted_iota(jnp.int32, packed.shape[1:], 1) < 64

    def one(i, carry):
        both = packed[i].astype(jnp.float32)
        turned = pltpu.roll(both, 64, 1)
        spread[2 * i] = jnp.where(left, both, turned).astype(jnp.bfloat16)
        spread[2 * i + 1] = jnp.where(left, turned, both).astype(jnp.bfloat16)
        return carry

    lax.fori_loop(0, packed.shape[0], one, 0)


def far_kernel(
    far_factor,
    coarse_factor,
    far_trips,
    far_owner,
    far_entry,
    far_words,
    coarse_trips,
    coarse_owner,
    coarse_entry,
    coarse_words,
    leaf_targets,
    leaf_packed,
    parent_targets,
    parent_packed,
    transfer,
    basis,
    near,
    out,
    leaf_spread,
    parent_spread,
    far_total,
    coarse_total,
):
    spread_halves(leaf_packed, leaf_spread)
    spread_halves(parent_packed, parent_spread)
    far_total[...] = jnp.zeros_like(far_total)
    coarse_total[...] = jnp.zeros_like(coarse_total)
    far_items(
        coarse_factor,
        coarse_trips,
        coarse_owner,
        coarse_entry,
        coarse_words,
        parent_targets,
        parent_spread,
        coarse_total,
    )
    far_items(
        far_factor, far_trips, far_owner, far_entry, far_words, leaf_targets, leaf_spread, far_total
    )
    leaves = basis.shape[0]
    size = basis.shape[2]
    for leaf in range(leaves):
        coarse = coarse_total[leaf // CH].astype(jnp.bfloat16)
        down = jnp.dot(coarse, transfer[leaf], preferred_element_type=jnp.float32)
        combined = (far_total[leaf] + down).astype(jnp.bfloat16)
        out[:, leaf * size : (leaf + 1) * size] = near[leaf] + jnp.dot(
            combined, basis[leaf], preferred_element_type=jnp.float32
        )


def per_device(
    coords,
    charges,
    leaf_basis,
    transfer,
    leaf_skeleton,
    parent_skeleton,
    near_ids,
    near_mask,
    far_ids,
    far_mask,
    coarse_ids,
    coarse_mask,
):
    leaves_dev, skeleton_size, leaf_size = leaf_basis.shape
    systems = charges.shape[0]
    parents_dev = leaves_dev // CH
    subs = lax.axis_size("sub")
    group_leaves = leaves_dev * subs
    first_leaf = lax.axis_index(("group", "sub")) * leaves_dev
    group_first = lax.axis_index("group") * group_leaves
    smem = pl.BlockSpec(memory_space=pltpu.SMEM)
    vmem = pl.BlockSpec(memory_space=pltpu.VMEM)

    own = jnp.concatenate([source_rows(coords), charges], axis=0)
    own = own.reshape(32, leaves_dev, leaf_size).transpose(1, 0, 2)
    up = [(i, i + 1) for i in range(subs - 1)]
    down = [(i + 1, i) for i in range(subs - 1)]
    before = lax.ppermute(own, "sub", up)
    after = lax.ppermute(own, "sub", down)

    leaf_coefs = jnp.einsum(
        "rlp,lkp->rlk",
        charges.reshape(systems, leaves_dev, leaf_size),
        leaf_basis,
        preferred_element_type=jnp.float32,
    ).astype(jnp.bfloat16)
    parent_coefs = jnp.einsum(
        "bckj,rbcj->rbk",
        transfer.reshape(parents_dev, CH, skeleton_size, skeleton_size),
        leaf_coefs.reshape(systems, parents_dev, CH, skeleton_size),
        preferred_element_type=jnp.float32,
    ).astype(jnp.bfloat16)

    def payload(skeleton, coefs):
        both = jnp.concatenate([source_rows(skeleton), coefs.reshape(systems, -1)], axis=0)
        return both.reshape(32, -1, 128).transpose(1, 0, 2)

    leaf_packed = lax.all_gather(payload(leaf_skeleton, leaf_coefs), "sub", axis=0, tiled=True)
    parent_packed = lax.all_gather(
        payload(parent_skeleton, parent_coefs), ("group", "sub"), axis=0, tiled=True
    )

    def columns(points, size):
        return target_rows(points).reshape(16, -1, size).transpose(1, 2, 0)

    near_targets = columns(coords, leaf_size)
    leaf_targets = columns(leaf_skeleton, skeleton_size)
    parent_targets = columns(parent_skeleton, skeleton_size)

    def lists(ids, mask, per_item, unroll):
        slots = -(-ids.shape[1] // per_item) * per_item
        extra = ((0, 0), (0, slots - ids.shape[1]))
        words, lengths = compact(jnp.pad(ids, extra), jnp.pad(mask, extra))
        owner, entry, trips = work_items(lengths, per_item, slots, unroll)
        return trips, owner, entry, jnp.pad(words.reshape(-1), (0, 128))

    near_lists = lists(near_ids - (first_leaf - leaves_dev), near_mask, 2, UNROLL_NEAR)
    far_lists = lists(far_ids - group_first, far_mask, 4, UNROLL_FAR)
    coarse_lists = lists(coarse_ids, coarse_mask, 4, UNROLL_FAR)

    near_sources = jnp.concatenate([before, own, after], axis=0)
    ln2 = 1.0 / LOG2E
    near = pl.pallas_call(
        functools.partial(near_kernel, ln2 / math.sqrt(near_ids.shape[1])),
        out_shape=jax.ShapeDtypeStruct((leaves_dev, systems, leaf_size), jnp.float32),
        in_specs=[smem] * 4 + [vmem] * 2,
        out_specs=vmem,
        cost_estimate=pl.CostEstimate(
            flops=20_000_000_000, bytes_accessed=4_000_000, transcendentals=20_000_000
        ),
        compiler_params=pltpu.CompilerParams(vmem_limit_bytes=40 * 2**20),
        name="near",
    )(*near_lists, near_targets, near_sources)

    return pl.pallas_call(
        functools.partial(
            far_kernel,
            ln2 / math.sqrt(far_ids.shape[1]),
            ln2 / math.sqrt(coarse_ids.shape[1]),
        ),
        out_shape=jax.ShapeDtypeStruct((systems, leaves_dev * leaf_size), jnp.float32),
        in_specs=[smem] * 8 + [vmem] * 7,
        out_specs=vmem,
        scratch_shapes=[
            pltpu.VMEM((2 * leaf_packed.shape[0], 32, 128), jnp.bfloat16),
            pltpu.VMEM((2 * parent_packed.shape[0], 32, 128), jnp.bfloat16),
            pltpu.VMEM((leaves_dev, systems, skeleton_size), jnp.float32),
            pltpu.VMEM((parents_dev, systems, skeleton_size), jnp.float32),
        ],
        compiler_params=pltpu.CompilerParams(vmem_limit_bytes=56 * 2**20),
        name="far",
    )(
        *far_lists,
        *coarse_lists,
        leaf_targets,
        leaf_packed,
        parent_targets,
        parent_packed,
        transfer,
        leaf_basis,
        near,
    )


def solution(mesh):
    placed = (
        P(None, ("group", "sub")),
        P(None, ("group", "sub")),
        P(("group", "sub"), None, None),
        P(("group", "sub"), None, None),
        P(None, ("group", "sub")),
        P(None, ("group", "sub")),
        P(("group", "sub"), None),
        P(("group", "sub"), None),
        P(("group", "sub"), None),
        P(("group", "sub"), None),
        P(("group", "sub"), None),
        P(("group", "sub"), None),
    )
    return jax.shard_map(
        per_device, mesh=mesh, in_specs=placed, out_specs=P(None, ("group", "sub")), check_vma=False
    )
```

```python
import functools
import math

import jax
import jax.numpy as jnp
from jax import lax
from jax.experimental import pallas as pl
from jax.experimental.pallas import tpu as pltpu
from jax.sharding import PartitionSpec as P

CH = 8
NEAR_UNROLL, NEAR_SLOTS = 16, 2
FAR_UNROLL, FAR_SLOTS = 16, 4
ZEROS_AT, ITEMS_AT = 100, 127
LOG2E = 1.4426950408889634
STRETCH = math.sqrt(3.0) / 0.25 * LOG2E


def split_points(points):
    def top(x):
        return x.astype(jnp.bfloat16).astype(jnp.float32)

    scaled = (points - 0.5) * STRETCH
    high = top(scaled)
    low = top(scaled - high)
    whole = high + low
    squares = whole * whole
    norm = squares[0:1] + squares[1:2] + squares[2:3]
    n1 = top(norm)
    n2 = top(norm - n1)
    return high, low, (n1, n2, norm - n1 - n2)


def fill_rows(points, sources, targets):
    high, low, norm = split_points(points)
    sources[...] = jnp.ones_like(sources)
    targets[...] = jnp.ones_like(targets)
    sources[0:3, :] = high
    sources[3:6, :] = high
    sources[6:9, :] = low
    targets[0:3, :] = -2.0 * high
    targets[3:6, :] = -2.0 * low
    targets[6:9, :] = -2.0 * high
    for i, piece in enumerate(norm):
        sources[12 + i : 13 + i, :] = piece
        targets[9 + i : 10 + i, :] = piece
    sources[15:16, :] = jnp.zeros_like(norm[0])


def prepare_kernel(
    coords,
    charges,
    basis,
    transfer,
    leaf_skeleton,
    parent_skeleton,
    near_out,
    far_out,
    near_targets,
    leaf_targets,
    parent_targets,
    rows_s,
    rows_t,
    coefs,
    parent_coefs,
):
    leaves, rank, size = basis.shape
    pairs = leaves * rank // 128

    def columns(out, width):
        for i in range(out.shape[0]):
            out[i] = rows_t[:, i * width : (i + 1) * width].T.astype(jnp.bfloat16)

    def block(rows, i):
        return rows[:, i * 128 : (i + 1) * 128].astype(jnp.bfloat16)

    for leaf in range(leaves):
        mine = lax.dot_general(
            charges[:, leaf * size : (leaf + 1) * size],
            basis[leaf],
            (((1,), (1,)), ((), ())),
            preferred_element_type=jnp.float32,
        )
        coefs[:, leaf * rank : (leaf + 1) * rank] = mine
    for parent in range(leaves // CH):
        total = jnp.zeros((charges.shape[0], rank), jnp.float32)
        for leaf in range(parent * CH, (parent + 1) * CH):
            total += lax.dot_general(
                coefs[:, leaf * rank : (leaf + 1) * rank].astype(jnp.bfloat16),
                transfer[leaf],
                (((1,), (1,)), ((), ())),
                preferred_element_type=jnp.float32,
            )
        parent_coefs[:, parent * rank : (parent + 1) * rank] = total

    def far_blocks(skeleton, values, first, count, targets):
        width = skeleton.shape[1]
        fill_rows(skeleton[...], rows_s.at[:, :width], rows_t.at[:, :width])
        for i in range(count):
            far_out[first + i, :16, :] = block(rows_s, i)
            far_out[first + i, 16:, :] = block(values, i)
        columns(targets, rank)

    far_blocks(leaf_skeleton, coefs, 0, pairs, leaf_targets)
    far_blocks(parent_skeleton, parent_coefs, pairs, pairs // CH, parent_targets)
    fill_rows(coords[...], rows_s, rows_t)
    for leaf in range(leaves):
        near_out[leaf, :16, :] = block(rows_s, leaf)
        near_out[leaf, 16:, :] = charges[:, leaf * size : (leaf + 1) * size]
    columns(near_targets, size)


def compact(ids, mask, per_item, words, items):
    rows, slots = ids.shape
    lane = lax.broadcasted_iota(jnp.int32, (rows, slots), 1)
    valid = mask != 0
    named = jnp.where(valid, ids, -1)
    count = jnp.zeros_like(ids)
    repeated = jnp.zeros_like(ids)
    for m in range(slots):
        same = jnp.where(ids == named[:, m : m + 1], 1, 0)
        count += same
        repeated += jnp.where(lane > m, same, 0)
    first = jnp.where(valid & (repeated == 0), 1, 0)
    ahead = jnp.where(
        lax.broadcasted_iota(jnp.int32, (slots, slots), 0)
        < lax.broadcasted_iota(jnp.int32, (slots, slots), 1),
        1.0,
        0.0,
    ).astype(jnp.bfloat16)
    place = jnp.dot(
        first.astype(jnp.float32).astype(jnp.bfloat16), ahead, preferred_element_type=jnp.float32
    ).astype(jnp.int32)
    packed = (ids * 128 + count) * first
    wide = lax.broadcasted_iota(jnp.int32, (rows, 128), 1)
    out = jnp.zeros((rows, 128), jnp.int32)
    for m in range(slots):
        out += jnp.where(wide == place[:, m : m + 1], packed[:, m : m + 1], 0)
    length = jnp.sum(first.astype(jnp.float32), axis=1, keepdims=True).astype(jnp.int32)
    blocks = jnp.broadcast_to((length + per_item - 1) // per_item, (rows, 128))
    until = jnp.where(
        lax.broadcasted_iota(jnp.int32, (rows, rows), 1)
        <= lax.broadcasted_iota(jnp.int32, (rows, rows), 0),
        1.0,
        0.0,
    )
    ends = jnp.dot(until, blocks.astype(jnp.float32), preferred_element_type=jnp.float32).astype(
        jnp.int32
    )
    starts = ends - blocks
    total = jnp.max(ends, axis=0, keepdims=True)
    words[...] = jnp.where(wide == ITEMS_AT, jnp.broadcast_to(total, (rows, 128)), out)
    for c in range(items.shape[0]):
        item = wide + c * 128
        owner = jnp.sum(jnp.where(item >= ends, 1, 0), axis=0, keepdims=True)
        start = jnp.max(jnp.where(item >= starts, starts, 0), axis=0, keepdims=True)
        entry = owner * 128 + (item[:1] - start) * per_item
        items[c : c + 1, :] = jnp.where(item[:1] < total, entry, (rows - 1) * 128 + ZEROS_AT)


def lists_kernel(near_ids, near_mask, far_ids, far_mask, coarse_ids, coarse_mask, *outs):
    compact(near_ids[...], near_mask[...], NEAR_SLOTS, outs[0], outs[1])
    compact(far_ids[...], far_mask[...], FAR_SLOTS, outs[2], outs[3])
    compact(coarse_ids[...], coarse_mask[...], FAR_SLOTS, outs[4], outs[5])


def tile_values(squared):
    squared = jnp.maximum(squared, 1e-12)
    u = (squared * lax.rsqrt(squared)).astype(jnp.bfloat16)
    return (u + jnp.bfloat16(LOG2E)) * jnp.exp2(-u)


def add_items(words, items, per_item, unroll, targets, fetch, total, factor):
    def entry(row, lane):
        word = words[row, lane]
        count = jnp.bitwise_and(word, 127).astype(jnp.float32).astype(jnp.bfloat16)
        return lax.shift_right_logical(word, 7), count

    def step(i, carry):
        rows, squared, values = [], [], []
        for k in range(unroll):
            item = i * unroll + k
            at = items[lax.shift_right_logical(item, 7), jnp.bitwise_and(item, 127)]
            row, lane = lax.shift_right_logical(at, 7), jnp.bitwise_and(at, 127)
            points, mine = fetch([entry(row, lane + s) for s in range(per_item)])
            rows.append(row)
            values.append(mine)
            squared.append(jnp.dot(targets[row], points, preferred_element_type=jnp.float32))
        tiles = [tile_values(s) for s in squared]
        sums = [
            lax.dot_general(v, t, (((1,), (1,)), ((), ())), preferred_element_type=jnp.float32)
            for v, t in zip(values, tiles)
        ]
        for row, part in zip(rows, sums):
            total[row] += factor * part
        return carry

    total[...] = jnp.zeros_like(total)
    lax.fori_loop(0, (words[0, ITEMS_AT] + unroll - 1) // unroll, step, 0)


def near_kernel(factor, words, items, targets, before, own, after, out, held):
    leaves = own.shape[0]
    for i, part in enumerate((before, own, after)):
        held[i * leaves : (i + 1) * leaves] = part[...]

    def fetch(entries):
        points = [held[i, :16, :] for i, _ in entries]
        values = [held[i, 16:, :] * c for i, c in entries]
        return jnp.concatenate(points, axis=1), jnp.concatenate(values, axis=1)

    add_items(words, items, NEAR_SLOTS, NEAR_UNROLL, targets, fetch, out, factor)


def fetch_halves(spread):
    left = lax.broadcasted_iota(jnp.int32, (16, 128), 1) < 64

    def fetch(entries):
        points, values = [], []
        for (ia, ca), (ib, cb) in zip(entries[::2], entries[1::2]):
            points.append(jnp.where(left, spread[ia, :16, :], spread[ib, :16, :]))
            values.append(jnp.where(left, spread[ia, 16:, :] * ca, spread[ib, 16:, :] * cb))
        return jnp.concatenate(points, axis=1), jnp.concatenate(values, axis=1)

    return fetch


def spread_halves(packed, spread, blocks, stride):
    left = lax.broadcasted_iota(jnp.int32, packed.shape[1:], 1) < 64

    def one(g, carry):
        for i in range(blocks):
            both = packed[g * stride + i].astype(jnp.float32)
            turned = pltpu.roll(both, 64, 1)
            at = 2 * (g * blocks + i)
            spread[at] = jnp.where(left, both, turned).astype(jnp.bfloat16)
            spread[at + 1] = jnp.where(left, turned, both).astype(jnp.bfloat16)
        return carry

    lax.fori_loop(0, packed.shape[0] // stride, one, 0)


def far_kernel(factor, blocks, stride, words, items, targets, packed, out, spread):
    spread_halves(packed, spread, blocks, stride)
    add_items(words, items, FAR_SLOTS, FAR_UNROLL, targets, fetch_halves(spread), out, factor)


def coarse_kernel(
    factor, words, items, targets, packed, transfer, basis, near, far, out, spread, total
):
    spread_halves(packed, spread, 2, 2)
    add_items(words, items, FAR_SLOTS, FAR_UNROLL, targets, fetch_halves(spread), total, factor)
    leaves, _, size = basis.shape
    for leaf in range(leaves):
        coarse = total[leaf // CH].astype(jnp.bfloat16)
        down = jnp.dot(coarse, transfer[leaf], preferred_element_type=jnp.float32)
        combined = (far[leaf] + down).astype(jnp.bfloat16)
        out[:, leaf * size : (leaf + 1) * size] = near[leaf] + jnp.dot(
            combined, basis[leaf], preferred_element_type=jnp.float32
        )


def per_device(
    coords,
    charges,
    leaf_basis,
    transfer,
    leaf_skeleton,
    parent_skeleton,
    near_ids,
    near_mask,
    far_ids,
    far_mask,
    coarse_ids,
    coarse_mask,
):
    leaves_dev, rank, leaf_size = leaf_basis.shape
    systems = charges.shape[0]
    parents_dev = leaves_dev // CH
    subs = lax.axis_size("sub")
    groups = lax.axis_size("group")
    group_leaves = leaves_dev * subs
    first_leaf = lax.axis_index(("group", "sub")) * leaves_dev
    group_first = lax.axis_index("group") * group_leaves
    smem = pl.BlockSpec(memory_space=pltpu.SMEM)
    vmem = pl.BlockSpec(memory_space=pltpu.VMEM)
    pairs = leaves_dev * rank // 128
    parent_pairs = parents_dev * rank // 128
    bf16, f32, i32 = jnp.bfloat16, jnp.float32, jnp.int32
    shape = jax.ShapeDtypeStruct

    def params(mib):
        return pltpu.CompilerParams(vmem_limit_bytes=mib * 2**20)

    own, packed, near_targets, leaf_targets, parent_targets = pl.pallas_call(
        prepare_kernel,
        out_shape=[
            shape((leaves_dev, 32, 128), bf16),
            shape((pairs + parent_pairs, 32, 128), bf16),
            shape((leaves_dev, leaf_size, 16), bf16),
            shape((leaves_dev, rank, 16), bf16),
            shape((parents_dev, rank, 16), bf16),
        ],
        in_specs=[vmem] * 6,
        out_specs=[vmem] * 5,
        scratch_shapes=[
            pltpu.VMEM((16, leaves_dev * leaf_size), f32),
            pltpu.VMEM((16, leaves_dev * leaf_size), f32),
            pltpu.VMEM((systems, leaves_dev * rank), f32),
            pltpu.VMEM((systems, parents_dev * rank), f32),
        ],
        compiler_params=params(40),
        name="prepare",
    )(coords, charges, leaf_basis, transfer, leaf_skeleton, parent_skeleton)

    before = lax.ppermute(own, "sub", [(i, i + 1) for i in range(subs - 1)])
    after = lax.ppermute(own, "sub", [(i + 1, i) for i in range(subs - 1)])
    group_packed = lax.all_gather(packed, "sub", axis=0, tiled=True)

    def item_rows(rows, slots, per_item):
        return -(-(rows * -(-slots // per_item) + 16) // 128)

    list_shapes = []
    for ids, per_item in ((near_ids, NEAR_SLOTS), (far_ids, FAR_SLOTS), (coarse_ids, FAR_SLOTS)):
        list_shapes.append(shape((ids.shape[0], 128), i32))
        list_shapes.append(shape((item_rows(*ids.shape, per_item), 128), i32))
    near_words, near_items, far_words, far_items, coarse_words, coarse_items = pl.pallas_call(
        lists_kernel,
        out_shape=list_shapes,
        in_specs=[vmem] * 6,
        out_specs=[vmem] * 6,
        compiler_params=params(40),
        name="lists",
    )(
        near_ids - (first_leaf - leaves_dev),
        near_mask,
        far_ids - group_first,
        far_mask,
        coarse_ids,
        coarse_mask,
    )

    cost = pl.CostEstimate(flops=20_000_000_000, bytes_accessed=4_000_000, transcendentals=20_000_000)
    ln2 = 1.0 / LOG2E
    near = pl.pallas_call(
        functools.partial(near_kernel, ln2 / math.sqrt(near_ids.shape[1])),
        out_shape=shape((leaves_dev, systems, leaf_size), f32),
        in_specs=[smem] * 2 + [vmem] * 4,
        out_specs=vmem,
        scratch_shapes=[pltpu.VMEM((3 * leaves_dev, 32, 128), bf16)],
        cost_estimate=cost,
        compiler_params=params(40),
        name="near",
    )(near_words, near_items, near_targets, before, own, after)

    near, group_packed = lax.optimization_barrier((near, group_packed))
    group_parents = group_packed.reshape(subs, pairs + parent_pairs, 32, 128)[:, pairs:]
    all_parents = lax.all_gather(
        group_parents.reshape(subs * parent_pairs, 32, 128), "group", axis=0, tiled=True
    )

    far = pl.pallas_call(
        functools.partial(
            far_kernel, ln2 / math.sqrt(far_ids.shape[1]), pairs, pairs + parent_pairs
        ),
        out_shape=shape((leaves_dev, systems, rank), f32),
        in_specs=[smem] * 2 + [vmem] * 2,
        out_specs=vmem,
        scratch_shapes=[pltpu.VMEM((group_leaves, 32, 128), bf16)],
        cost_estimate=cost,
        compiler_params=params(40),
        name="far",
    )(far_words, far_items, leaf_targets, group_packed)

    return pl.pallas_call(
        functools.partial(coarse_kernel, ln2 / math.sqrt(coarse_ids.shape[1])),
        out_shape=shape((systems, leaves_dev * leaf_size), f32),
        in_specs=[smem] * 2 + [vmem] * 6,
        out_specs=vmem,
        scratch_shapes=[
            pltpu.VMEM((groups * subs * parents_dev, 32, 128), bf16),
            pltpu.VMEM((parents_dev, systems, rank), f32),
        ],
        compiler_params=params(56),
        name="coarse",
    )(
        coarse_words,
        coarse_items,
        parent_targets,
        all_parents,
        transfer,
        leaf_basis,
        near,
        far,
    )


def solution(mesh):
    placed = (
        P(None, ("group", "sub")),
        P(None, ("group", "sub")),
        P(("group", "sub"), None, None),
        P(("group", "sub"), None, None),
        P(None, ("group", "sub")),
        P(None, ("group", "sub")),
        P(("group", "sub"), None),
        P(("group", "sub"), None),
        P(("group", "sub"), None),
        P(("group", "sub"), None),
        P(("group", "sub"), None),
        P(("group", "sub"), None),
    )
    return jax.shard_map(
        per_device, mesh=mesh, in_specs=placed, out_specs=P(None, ("group", "sub")), check_vma=False
    )
```

```python
import functools
import math

import jax
import jax.numpy as jnp
from jax import lax
from jax.experimental import pallas as pl
from jax.experimental.pallas import tpu as pltpu
from jax.sharding import PartitionSpec as P

CH = 8
NEAR_UNROLL, NEAR_SLOTS = 16, 2
FAR_UNROLL, FAR_SLOTS = 16, 4
ZEROS_AT, ITEMS_AT = 100, 127
LOG2E = 1.4426950408889634
STRETCH = math.sqrt(3.0) / 0.25 * LOG2E


def split_points(points):
    def top(x):
        return x.astype(jnp.bfloat16).astype(jnp.float32)

    scaled = (points - 0.5) * STRETCH
    high = top(scaled)
    low = top(scaled - high)
    whole = high + low
    squares = whole * whole
    norm = squares[0:1] + squares[1:2] + squares[2:3]
    n1 = top(norm)
    n2 = top(norm - n1)
    return high, low, (n1, n2, norm - n1 - n2)


def fill_rows(points, sources, targets):
    high, low, norm = split_points(points)
    sources[...] = jnp.ones_like(sources)
    targets[...] = jnp.ones_like(targets)
    sources[0:3, :] = high
    sources[3:6, :] = high
    sources[6:9, :] = low
    targets[0:3, :] = -2.0 * high
    targets[3:6, :] = -2.0 * low
    targets[6:9, :] = -2.0 * high
    for i, piece in enumerate(norm):
        sources[12 + i : 13 + i, :] = piece
        targets[9 + i : 10 + i, :] = piece
    sources[15:16, :] = jnp.zeros_like(norm[0])


def prepare_kernel(
    coords,
    charges,
    basis,
    transfer,
    leaf_skeleton,
    parent_skeleton,
    near_out,
    far_out,
    near_targets,
    leaf_targets,
    parent_targets,
    rows_s,
    rows_t,
    coefs,
    parent_coefs,
):
    leaves, rank, size = basis.shape
    pairs = leaves * rank // 128

    def columns(out, width):
        for i in range(out.shape[0]):
            out[i] = rows_t[:, i * width : (i + 1) * width].T.astype(jnp.bfloat16)

    def block(rows, i):
        return rows[:, i * 128 : (i + 1) * 128].astype(jnp.bfloat16)

    for leaf in range(leaves):
        mine = lax.dot_general(
            charges[:, leaf * size : (leaf + 1) * size],
            basis[leaf],
            (((1,), (1,)), ((), ())),
            preferred_element_type=jnp.float32,
        )
        coefs[:, leaf * rank : (leaf + 1) * rank] = mine
    for parent in range(leaves // CH):
        total = jnp.zeros((charges.shape[0], rank), jnp.float32)
        for leaf in range(parent * CH, (parent + 1) * CH):
            total += lax.dot_general(
                coefs[:, leaf * rank : (leaf + 1) * rank].astype(jnp.bfloat16),
                transfer[leaf],
                (((1,), (1,)), ((), ())),
                preferred_element_type=jnp.float32,
            )
        parent_coefs[:, parent * rank : (parent + 1) * rank] = total

    def far_blocks(skeleton, values, first, count, targets):
        width = skeleton.shape[1]
        fill_rows(skeleton[...], rows_s.at[:, :width], rows_t.at[:, :width])
        for i in range(count):
            far_out[first + i, :16, :] = block(rows_s, i)
            far_out[first + i, 16:, :] = block(values, i)
        columns(targets, rank)

    far_blocks(leaf_skeleton, coefs, 0, pairs, leaf_targets)
    far_blocks(parent_skeleton, parent_coefs, pairs, pairs // CH, parent_targets)
    fill_rows(coords[...], rows_s, rows_t)
    for leaf in range(leaves):
        near_out[leaf, :16, :] = block(rows_s, leaf)
        near_out[leaf, 16:, :] = charges[:, leaf * size : (leaf + 1) * size]
    columns(near_targets, size)


def compact(ids, mask, per_item, words, items):
    rows, slots = ids.shape
    lane = lax.broadcasted_iota(jnp.int32, (rows, slots), 1)
    valid = mask != 0
    named = jnp.where(valid, ids, -1)
    count = jnp.zeros_like(ids)
    repeated = jnp.zeros_like(ids)
    for m in range(slots):
        same = jnp.where(ids == named[:, m : m + 1], 1, 0)
        count += same
        repeated += jnp.where(lane > m, same, 0)
    first = jnp.where(valid & (repeated == 0), 1, 0)
    ahead = jnp.where(
        lax.broadcasted_iota(jnp.int32, (slots, slots), 0)
        < lax.broadcasted_iota(jnp.int32, (slots, slots), 1),
        1.0,
        0.0,
    ).astype(jnp.bfloat16)
    place = jnp.dot(
        first.astype(jnp.float32).astype(jnp.bfloat16), ahead, preferred_element_type=jnp.float32
    ).astype(jnp.int32)
    packed = (ids * 128 + count) * first
    wide = lax.broadcasted_iota(jnp.int32, (rows, 128), 1)
    out = jnp.zeros((rows, 128), jnp.int32)
    for m in range(slots):
        out += jnp.where(wide == place[:, m : m + 1], packed[:, m : m + 1], 0)
    length = jnp.sum(first.astype(jnp.float32), axis=1, keepdims=True).astype(jnp.int32)
    blocks = jnp.broadcast_to((length + per_item - 1) // per_item, (rows, 128))
    until = jnp.where(
        lax.broadcasted_iota(jnp.int32, (rows, rows), 1)
        <= lax.broadcasted_iota(jnp.int32, (rows, rows), 0),
        1.0,
        0.0,
    )
    ends = jnp.dot(until, blocks.astype(jnp.float32), preferred_element_type=jnp.float32).astype(
        jnp.int32
    )
    starts = ends - blocks
    total = jnp.max(ends, axis=0, keepdims=True)
    words[...] = jnp.where(wide == ITEMS_AT, jnp.broadcast_to(total, (rows, 128)), out)
    for c in range(items.shape[0]):
        item = wide + c * 128
        owner = jnp.sum(jnp.where(item >= ends, 1, 0), axis=0, keepdims=True)
        start = jnp.max(jnp.where(item >= starts, starts, 0), axis=0, keepdims=True)
        entry = owner * 128 + (item[:1] - start) * per_item
        items[c : c + 1, :] = jnp.where(item[:1] < total, entry, (rows - 1) * 128 + ZEROS_AT)


def lists_kernel(near_ids, near_mask, far_ids, far_mask, coarse_ids, coarse_mask, *outs):
    compact(near_ids[...], near_mask[...], NEAR_SLOTS, outs[0], outs[1])
    compact(far_ids[...], far_mask[...], FAR_SLOTS, outs[2], outs[3])
    compact(coarse_ids[...], coarse_mask[...], FAR_SLOTS, outs[4], outs[5])


def tile_values(squared):
    squared = jnp.maximum(squared, 1e-12)
    u = squared * lax.rsqrt(squared)
    return ((u + LOG2E) * jnp.exp2(-u)).astype(jnp.bfloat16)


def add_items(words, items, per_item, unroll, targets, fetch, total, factor):
    def entry(row, lane):
        word = words[row, lane]
        count = jnp.bitwise_and(word, 127).astype(jnp.float32).astype(jnp.bfloat16)
        return lax.shift_right_logical(word, 7), count

    def step(i, carry):
        rows, squared, values = [], [], []
        for k in range(unroll):
            item = i * unroll + k
            at = items[lax.shift_right_logical(item, 7), jnp.bitwise_and(item, 127)]
            row, lane = lax.shift_right_logical(at, 7), jnp.bitwise_and(at, 127)
            points, mine = fetch([entry(row, lane + s) for s in range(per_item)])
            rows.append(row)
            values.append(mine)
            squared.append(jnp.dot(targets[row], points, preferred_element_type=jnp.float32))
        tiles = [tile_values(s) for s in squared]
        sums = [
            lax.dot_general(v, t, (((1,), (1,)), ((), ())), preferred_element_type=jnp.float32)
            for v, t in zip(values, tiles)
        ]
        for row, part in zip(rows, sums):
            total[row] += factor * part
        return carry

    total[...] = jnp.zeros_like(total)
    lax.fori_loop(0, (words[0, ITEMS_AT] + unroll - 1) // unroll, step, 0)


def exchange_kernel(
    subs, groups, pairs, own, packed, before, after, joined, send, recv, local, near_sends
):
    sub, group = lax.axis_index("sub"), lax.axis_index("group")
    right, left = lax.rem(sub + 1, subs), lax.rem(sub + subs - 1, subs)
    mesh_id = pl.DeviceIdType.MESH
    partners = [(group, right), (group, left)]
    partners += [(lax.rem(group + groups - d, groups), sub) for d in range(1, groups)]
    barrier = pltpu.get_barrier_semaphore()
    for partner in partners:
        pl.semaphore_signal(barrier, inc=1, device_id=partner, device_id_type=mesh_id)
    mine = packed.shape[0]
    keep = pltpu.make_async_copy(packed, joined.at[pl.ds(0, mine)], local)
    keep.start()
    pl.semaphore_wait(barrier, len(partners))
    width = mine - pairs
    copies = []
    for k, partner in enumerate(partners[2:]):
        copies.append(
            pltpu.make_async_remote_copy(
                src_ref=packed.at[pl.ds(pairs, width)],
                dst_ref=joined.at[pl.ds(pairs + (k + 1) * width, width)],
                send_sem=send.at[k],
                recv_sem=recv.at[k],
                device_id=partner,
                device_id_type=mesh_id,
            )
        )
        copies[-1].start()
    for k, landing in enumerate((before, after)):
        copies.append(
            pltpu.make_async_remote_copy(
                src_ref=own,
                dst_ref=landing,
                send_sem=near_sends.at[k],
                recv_sem=near_sends.at[2 + k],
                device_id=partners[k],
                device_id_type=mesh_id,
            )
        )
        copies[-1].start()
    for copy in copies:
        copy.wait()
    keep.wait()


def near_kernel(factor, words, items, targets, before, own, after, out, held):
    leaves = own.shape[0]
    for i, part in enumerate((before, own, after)):
        held[i * leaves : (i + 1) * leaves] = part[...]

    def fetch(entries):
        points = [held[i, :16, :] for i, _ in entries]
        values = [held[i, 16:, :] * c for i, c in entries]
        return jnp.concatenate(points, axis=1), jnp.concatenate(values, axis=1)

    add_items(words, items, NEAR_SLOTS, NEAR_UNROLL, targets, fetch, out, factor)


def fetch_halves(spread):
    left = lax.broadcasted_iota(jnp.int32, (16, 128), 1) < 64

    def fetch(entries):
        points, values = [], []
        for (ia, ca), (ib, cb) in zip(entries[::2], entries[1::2]):
            points.append(jnp.where(left, spread[ia, :16, :], spread[ib, :16, :]))
            values.append(jnp.where(left, spread[ia, 16:, :] * ca, spread[ib, 16:, :] * cb))
        return jnp.concatenate(points, axis=1), jnp.concatenate(values, axis=1)

    return fetch


def spread_halves(packed, spread, offset, blocks, stride):
    left = lax.broadcasted_iota(jnp.int32, packed.shape[1:], 1) < 64

    def one(g, carry):
        for i in range(blocks):
            both = packed[g * stride + offset + i].astype(jnp.float32)
            turned = pltpu.roll(both, 64, 1)
            at = 2 * (g * blocks + i)
            spread[at] = jnp.where(left, both, turned).astype(jnp.bfloat16)
            spread[at + 1] = jnp.where(left, turned, both).astype(jnp.bfloat16)
        return carry

    lax.fori_loop(0, packed.shape[0] // stride, one, 0)


def far_kernel(
    far_factor,
    coarse_factor,
    pairs,
    stride,
    far_words,
    far_items,
    coarse_words,
    coarse_items,
    leaf_targets,
    parent_targets,
    packed,
    transfer,
    basis,
    near,
    out,
    leaf_spread,
    parent_spread,
    far,
    total,
):
    spread_halves(packed, parent_spread, pairs, stride - pairs, stride)
    spread_halves(packed, leaf_spread, 0, pairs, stride)
    add_items(
        coarse_words,
        coarse_items,
        FAR_SLOTS,
        FAR_UNROLL,
        parent_targets,
        fetch_halves(parent_spread),
        total,
        coarse_factor,
    )
    add_items(
        far_words,
        far_items,
        FAR_SLOTS,
        FAR_UNROLL,
        leaf_targets,
        fetch_halves(leaf_spread),
        far,
        far_factor,
    )
    leaves, _, size = basis.shape
    for leaf in range(leaves):
        coarse = total[leaf // CH].astype(jnp.bfloat16)
        down = jnp.dot(coarse, transfer[leaf], preferred_element_type=jnp.float32)
        combined = (far[leaf] + down).astype(jnp.bfloat16)
        out[:, leaf * size : (leaf + 1) * size] = near[leaf] + jnp.dot(
            combined, basis[leaf], preferred_element_type=jnp.float32
        )


def per_device(
    coords,
    charges,
    leaf_basis,
    transfer,
    leaf_skeleton,
    parent_skeleton,
    near_ids,
    near_mask,
    far_ids,
    far_mask,
    coarse_ids,
    coarse_mask,
):
    leaves_dev, rank, leaf_size = leaf_basis.shape
    systems = charges.shape[0]
    parents_dev = leaves_dev // CH
    subs = lax.axis_size("sub")
    groups = lax.axis_size("group")
    group_leaves = leaves_dev * subs
    first_leaf = lax.axis_index(("group", "sub")) * leaves_dev
    group_first = lax.axis_index("group") * group_leaves
    smem = pl.BlockSpec(memory_space=pltpu.SMEM)
    vmem = pl.BlockSpec(memory_space=pltpu.VMEM)
    pairs = leaves_dev * rank // 128
    parent_pairs = parents_dev * rank // 128
    bf16, f32, i32 = jnp.bfloat16, jnp.float32, jnp.int32
    shape = jax.ShapeDtypeStruct

    def params(mib):
        return pltpu.CompilerParams(vmem_limit_bytes=mib * 2**20)

    own, packed, near_targets, leaf_targets, parent_targets = pl.pallas_call(
        prepare_kernel,
        out_shape=[
            shape((leaves_dev, 32, 128), bf16),
            shape((pairs + parent_pairs, 32, 128), bf16),
            shape((leaves_dev, leaf_size, 16), bf16),
            shape((leaves_dev, rank, 16), bf16),
            shape((parents_dev, rank, 16), bf16),
        ],
        in_specs=[vmem] * 6,
        out_specs=[vmem] * 5,
        scratch_shapes=[
            pltpu.VMEM((16, leaves_dev * leaf_size), f32),
            pltpu.VMEM((16, leaves_dev * leaf_size), f32),
            pltpu.VMEM((systems, leaves_dev * rank), f32),
            pltpu.VMEM((systems, parents_dev * rank), f32),
        ],
        compiler_params=params(40),
        name="prepare",
    )(coords, charges, leaf_basis, transfer, leaf_skeleton, parent_skeleton)

    stride = pairs + groups * parent_pairs
    before, after, joined = pl.pallas_call(
        functools.partial(exchange_kernel, subs, groups, pairs),
        out_shape=[shape(own.shape, bf16)] * 2 + [shape((stride, 32, 128), bf16)],
        in_specs=[vmem] * 2,
        out_specs=[vmem] * 3,
        scratch_shapes=[
            pltpu.SemaphoreType.DMA((groups - 1,)),
            pltpu.SemaphoreType.DMA((groups - 1,)),
            pltpu.SemaphoreType.DMA,
            pltpu.SemaphoreType.DMA((4,)),
        ],
        compiler_params=pltpu.CompilerParams(
            vmem_limit_bytes=16 * 2**20, collective_id=0, has_side_effects=True
        ),
        name="exchange",
    )(own, packed)
    group_packed = lax.all_gather(joined, "sub", axis=0, tiled=True)

    everyone = groups * subs * parents_dev
    ahead = lax.rem(
        coarse_ids - lax.axis_index("group") * (subs * parents_dev) + everyone, everyone
    )
    inside = lax.rem(ahead, subs * parents_dev)
    coarse_at = (
        (inside // parents_dev) * (groups * parents_dev)
        + (ahead // (subs * parents_dev)) * parents_dev
        + lax.rem(inside, parents_dev)
    )

    def item_rows(rows, slots, per_item):
        return -(-(rows * -(-slots // per_item) + 16) // 128)

    list_shapes = []
    for ids, per_item in ((near_ids, NEAR_SLOTS), (far_ids, FAR_SLOTS), (coarse_ids, FAR_SLOTS)):
        list_shapes.append(shape((ids.shape[0], 128), i32))
        list_shapes.append(shape((item_rows(*ids.shape, per_item), 128), i32))
    near_words, near_items, far_words, far_items, coarse_words, coarse_items = pl.pallas_call(
        lists_kernel,
        out_shape=list_shapes,
        in_specs=[vmem] * 6,
        out_specs=[vmem] * 6,
        compiler_params=params(40),
        name="lists",
    )(
        near_ids - (first_leaf - leaves_dev),
        near_mask,
        far_ids - group_first,
        far_mask,
        coarse_at,
        coarse_mask,
    )

    cost = pl.CostEstimate(flops=20_000_000_000, bytes_accessed=4_000_000, transcendentals=20_000_000)
    ln2 = 1.0 / LOG2E
    near = pl.pallas_call(
        functools.partial(near_kernel, ln2 / math.sqrt(near_ids.shape[1])),
        out_shape=shape((leaves_dev, systems, leaf_size), f32),
        in_specs=[smem] * 2 + [vmem] * 4,
        out_specs=vmem,
        scratch_shapes=[pltpu.VMEM((3 * leaves_dev, 32, 128), bf16)],
        cost_estimate=cost,
        compiler_params=params(40),
        name="near",
    )(near_words, near_items, near_targets, before, own, after)

    return pl.pallas_call(
        functools.partial(
            far_kernel,
            ln2 / math.sqrt(far_ids.shape[1]),
            ln2 / math.sqrt(coarse_ids.shape[1]),
            pairs,
            stride,
        ),
        out_shape=shape((systems, leaves_dev * leaf_size), f32),
        in_specs=[smem] * 4 + [vmem] * 6,
        out_specs=vmem,
        scratch_shapes=[
            pltpu.VMEM((group_leaves, 32, 128), bf16),
            pltpu.VMEM((everyone, 32, 128), bf16),
            pltpu.VMEM((leaves_dev, systems, rank), f32),
            pltpu.VMEM((parents_dev, systems, rank), f32),
        ],
        compiler_params=params(56),
        name="far",
    )(
        far_words,
        far_items,
        coarse_words,
        coarse_items,
        leaf_targets,
        parent_targets,
        group_packed,
        transfer,
        leaf_basis,
        near,
    )


def solution(mesh):
    placed = (
        P(None, ("group", "sub")),
        P(None, ("group", "sub")),
        P(("group", "sub"), None, None),
        P(("group", "sub"), None, None),
        P(None, ("group", "sub")),
        P(None, ("group", "sub")),
        P(("group", "sub"), None),
        P(("group", "sub"), None),
        P(("group", "sub"), None),
        P(("group", "sub"), None),
        P(("group", "sub"), None),
        P(("group", "sub"), None),
    )
    return jax.shard_map(
        per_device, mesh=mesh, in_specs=placed, out_specs=P(None, ("group", "sub")), check_vma=False
    )
```

```python
import functools
import math

import jax
import jax.numpy as jnp
from jax import lax
from jax.experimental import pallas as pl
from jax.experimental.pallas import tpu as pltpu
from jax.sharding import PartitionSpec as P

CH = 8
NEAR_UNROLL, NEAR_SLOTS = 16, 2
FAR_UNROLL, FAR_SLOTS = 16, 4
ZEROS_AT, ITEMS_AT = 100, 127
LOG2E = 1.4426950408889634
STRETCH = math.sqrt(3.0) / 0.25 * LOG2E


def split_points(points):
    def top(x):
        return x.astype(jnp.bfloat16).astype(jnp.float32)

    scaled = (points - 0.5) * STRETCH
    high = top(scaled)
    low = top(scaled - high)
    whole = high + low
    squares = whole * whole
    norm = squares[0:1] + squares[1:2] + squares[2:3]
    n1 = top(norm)
    n2 = top(norm - n1)
    return high, low, (n1, n2, norm - n1 - n2)


def fill_rows(points, sources, targets):
    high, low, norm = split_points(points)
    sources[...] = jnp.ones_like(sources)
    targets[...] = jnp.ones_like(targets)
    sources[0:3, :] = high
    sources[3:6, :] = high
    sources[6:9, :] = low
    targets[0:3, :] = -2.0 * high
    targets[3:6, :] = -2.0 * low
    targets[6:9, :] = -2.0 * high
    for i, piece in enumerate(norm):
        sources[12 + i : 13 + i, :] = piece
        targets[9 + i : 10 + i, :] = piece
    sources[15:16, :] = jnp.zeros_like(norm[0])


def prepare_kernel(
    subs,
    groups,
    coords_in,
    charges_in,
    basis_in,
    transfer_in,
    leaf_skeleton_in,
    parent_skeleton_in,
    near_out,
    joined,
    near_targets,
    leaf_targets,
    parent_targets,
    points,
    values,
    basis,
    transfer,
    leaf_skeleton,
    parent_skeleton,
    rows_s,
    rows_t,
    coefs,
    parent_coefs,
    loads,
    halo_send,
    halo_recv,
    send,
    recv,
):
    leaves, rank, size = basis.shape
    pairs = leaves * rank // 128
    width = pairs // CH
    sub, group = lax.axis_index("sub"), lax.axis_index("group")
    right, left = lax.rem(sub + 1, subs), lax.rem(sub + subs - 1, subs)
    mesh_id = pl.DeviceIdType.MESH
    sides = [(group, right), (group, left)]
    partners = [(lax.rem(group + groups - d, groups), sub) for d in range(1, groups)]
    barrier = pltpu.get_barrier_semaphore()
    for partner in sides + partners:
        pl.semaphore_signal(barrier, inc=1, device_id=partner, device_id_type=mesh_id)
    moves = [
        (charges_in, values.at[0]),
        (basis_in, basis),
        (transfer_in, transfer),
        (parent_skeleton_in, parent_skeleton),
        (leaf_skeleton_in, leaf_skeleton),
        (coords_in, points.at[0]),
    ]
    held = [pltpu.make_async_copy(a, b, loads.at[i]) for i, (a, b) in enumerate(moves)]
    for copy in held:
        copy.start()
    pl.semaphore_wait(barrier, len(sides) + len(partners))
    halo = []
    for k, side in enumerate(sides):
        for n, (source, landing) in enumerate(((coords_in, points), (charges_in, values))):
            halo.append(
                pltpu.make_async_remote_copy(
                    src_ref=source,
                    dst_ref=landing.at[1 + k],
                    send_sem=halo_send.at[2 * k + n],
                    recv_sem=halo_recv.at[2 * k + n],
                    device_id=side,
                    device_id_type=mesh_id,
                )
            )
            halo[-1].start()

    def columns(out, width):
        for i in range(out.shape[0]):
            out[i] = rows_t[:, i * width : (i + 1) * width].T.astype(jnp.bfloat16)

    def block(rows, i):
        return rows[:, i * 128 : (i + 1) * 128].astype(jnp.bfloat16)

    for copy in held[:3]:
        copy.wait()
    for leaf in range(leaves):
        mine = lax.dot_general(
            values[0, :, leaf * size : (leaf + 1) * size],
            basis[leaf],
            (((1,), (1,)), ((), ())),
            preferred_element_type=jnp.float32,
        )
        coefs[:, leaf * rank : (leaf + 1) * rank] = mine
    for parent in range(leaves // CH):
        total = jnp.zeros((coefs.shape[0], rank), jnp.float32)
        for leaf in range(parent * CH, (parent + 1) * CH):
            total += lax.dot_general(
                coefs[:, leaf * rank : (leaf + 1) * rank].astype(jnp.bfloat16),
                transfer[leaf],
                (((1,), (1,)), ((), ())),
                preferred_element_type=jnp.float32,
            )
        parent_coefs[:, parent * rank : (parent + 1) * rank] = total

    def far_blocks(skeleton, numbers, first, count, targets):
        lanes = skeleton.shape[1]
        fill_rows(skeleton[...], rows_s.at[:, :lanes], rows_t.at[:, :lanes])
        for i in range(count):
            joined[first + i, :16, :] = block(rows_s, i)
            joined[first + i, 16:, :] = block(numbers, i)
        columns(targets, rank)

    held[3].wait()
    far_blocks(parent_skeleton, parent_coefs, pairs, width, parent_targets)
    across = []
    for k, partner in enumerate(partners):
        across.append(
            pltpu.make_async_remote_copy(
                src_ref=joined.at[pl.ds(pairs, width)],
                dst_ref=joined.at[pl.ds(pairs + (k + 1) * width, width)],
                send_sem=send.at[k],
                recv_sem=recv.at[k],
                device_id=partner,
                device_id_type=mesh_id,
            )
        )
        across[-1].start()
    held[4].wait()
    far_blocks(leaf_skeleton, coefs, 0, pairs, leaf_targets)

    def near_blocks(part, first):
        fill_rows(points[part], rows_s, rows_t)
        for leaf in range(leaves):
            near_out[first + leaf, :16, :] = block(rows_s, leaf)
            near_out[first + leaf, 16:, :] = values[part, :, leaf * size : (leaf + 1) * size]

    held[5].wait()
    near_blocks(0, leaves)
    columns(near_targets, size)
    for copy in halo[:2]:
        copy.wait()
    near_blocks(1, 0)
    for copy in halo[2:]:
        copy.wait()
    near_blocks(2, 2 * leaves)
    for copy in across:
        copy.wait()


def compact(ids, mask, per_item, words, items):
    rows, slots = ids.shape
    lane = lax.broadcasted_iota(jnp.int32, (rows, slots), 1)
    valid = mask != 0
    named = jnp.where(valid, ids, -1)
    count = jnp.zeros_like(ids)
    repeated = jnp.zeros_like(ids)
    for m in range(slots):
        same = jnp.where(ids == named[:, m : m + 1], 1, 0)
        count += same
        repeated += jnp.where(lane > m, same, 0)
    first = jnp.where(valid & (repeated == 0), 1, 0)
    ahead = jnp.where(
        lax.broadcasted_iota(jnp.int32, (slots, slots), 0)
        < lax.broadcasted_iota(jnp.int32, (slots, slots), 1),
        1.0,
        0.0,
    ).astype(jnp.bfloat16)
    place = jnp.dot(
        first.astype(jnp.float32).astype(jnp.bfloat16), ahead, preferred_element_type=jnp.float32
    ).astype(jnp.int32)
    packed = (ids * 128 + count) * first
    wide = lax.broadcasted_iota(jnp.int32, (rows, 128), 1)
    out = jnp.zeros((rows, 128), jnp.int32)
    for m in range(slots):
        out += jnp.where(wide == place[:, m : m + 1], packed[:, m : m + 1], 0)
    length = jnp.sum(first.astype(jnp.float32), axis=1, keepdims=True).astype(jnp.int32)
    blocks = jnp.broadcast_to((length + per_item - 1) // per_item, (rows, 128))
    until = jnp.where(
        lax.broadcasted_iota(jnp.int32, (rows, rows), 1)
        <= lax.broadcasted_iota(jnp.int32, (rows, rows), 0),
        1.0,
        0.0,
    )
    ends = jnp.dot(until, blocks.astype(jnp.float32), preferred_element_type=jnp.float32).astype(
        jnp.int32
    )
    starts = ends - blocks
    total = jnp.max(ends, axis=0, keepdims=True)
    words[...] = jnp.where(wide == ITEMS_AT, jnp.broadcast_to(total, (rows, 128)), out)
    for c in range(items.shape[0]):
        item = wide + c * 128
        owner = jnp.sum(jnp.where(item >= ends, 1, 0), axis=0, keepdims=True)
        start = jnp.max(jnp.where(item >= starts, starts, 0), axis=0, keepdims=True)
        entry = owner * 128 + (item[:1] - start) * per_item
        items[c : c + 1, :] = jnp.where(item[:1] < total, entry, (rows - 1) * 128 + ZEROS_AT)


def lists_kernel(near_ids, near_mask, far_ids, far_mask, coarse_ids, coarse_mask, *outs):
    compact(near_ids[...], near_mask[...], NEAR_SLOTS, outs[0], outs[1])
    compact(far_ids[...], far_mask[...], FAR_SLOTS, outs[2], outs[3])
    compact(coarse_ids[...], coarse_mask[...], FAR_SLOTS, outs[4], outs[5])


def tile_values(squared):
    squared = jnp.maximum(squared, 1e-12)
    u = squared * lax.rsqrt(squared)
    return ((u + LOG2E) * jnp.exp2(-u)).astype(jnp.bfloat16)


def add_items(words, items, per_item, unroll, targets, fetch, total, factor):
    def entry(row, lane):
        word = words[row, lane]
        count = jnp.bitwise_and(word, 127).astype(jnp.float32).astype(jnp.bfloat16)
        return lax.shift_right_logical(word, 7), count

    def step(i, carry):
        rows, squared, values = [], [], []
        for k in range(unroll):
            item = i * unroll + k
            at = items[lax.shift_right_logical(item, 7), jnp.bitwise_and(item, 127)]
            row, lane = lax.shift_right_logical(at, 7), jnp.bitwise_and(at, 127)
            points, mine = fetch([entry(row, lane + s) for s in range(per_item)])
            rows.append(row)
            values.append(mine)
            squared.append(jnp.dot(targets[row], points, preferred_element_type=jnp.float32))
        tiles = [tile_values(s) for s in squared]
        sums = [
            lax.dot_general(v, t, (((1,), (1,)), ((), ())), preferred_element_type=jnp.float32)
            for v, t in zip(values, tiles)
        ]
        for row, part in zip(rows, sums):
            total[row] += factor * part
        return carry

    total[...] = jnp.zeros_like(total)
    lax.fori_loop(0, (words[0, ITEMS_AT] + unroll - 1) // unroll, step, 0)


def near_kernel(factor, words, items, targets, held, out):
    def fetch(entries):
        points = [held[i, :16, :] for i, _ in entries]
        values = [held[i, 16:, :] * c for i, c in entries]
        return jnp.concatenate(points, axis=1), jnp.concatenate(values, axis=1)

    add_items(words, items, NEAR_SLOTS, NEAR_UNROLL, targets, fetch, out, factor)


def fetch_halves(spread):
    left = lax.broadcasted_iota(jnp.int32, (16, 128), 1) < 64

    def fetch(entries):
        points, values = [], []
        for (ia, ca), (ib, cb) in zip(entries[::2], entries[1::2]):
            points.append(jnp.where(left, spread[ia, :16, :], spread[ib, :16, :]))
            values.append(jnp.where(left, spread[ia, 16:, :] * ca, spread[ib, 16:, :] * cb))
        return jnp.concatenate(points, axis=1), jnp.concatenate(values, axis=1)

    return fetch


def spread_halves(packed, spread, offset, blocks, stride):
    left = lax.broadcasted_iota(jnp.int32, packed.shape[1:], 1) < 64

    def one(g, carry):
        for i in range(blocks):
            both = packed[g * stride + offset + i].astype(jnp.float32)
            turned = pltpu.roll(both, 64, 1)
            at = 2 * (g * blocks + i)
            spread[at] = jnp.where(left, both, turned).astype(jnp.bfloat16)
            spread[at + 1] = jnp.where(left, turned, both).astype(jnp.bfloat16)
        return carry

    lax.fori_loop(0, packed.shape[0] // stride, one, 0)


def far_kernel(
    far_factor,
    coarse_factor,
    pairs,
    stride,
    far_words,
    far_items,
    coarse_words,
    coarse_items,
    leaf_targets,
    parent_targets,
    packed,
    transfer,
    basis,
    near,
    out,
    leaf_spread,
    parent_spread,
    far,
    total,
):
    spread_halves(packed, parent_spread, pairs, stride - pairs, stride)
    spread_halves(packed, leaf_spread, 0, pairs, stride)
    add_items(
        coarse_words,
        coarse_items,
        FAR_SLOTS,
        FAR_UNROLL,
        parent_targets,
        fetch_halves(parent_spread),
        total,
        coarse_factor,
    )
    add_items(
        far_words,
        far_items,
        FAR_SLOTS,
        FAR_UNROLL,
        leaf_targets,
        fetch_halves(leaf_spread),
        far,
        far_factor,
    )
    leaves, _, size = basis.shape
    for leaf in range(leaves):
        coarse = total[leaf // CH].astype(jnp.bfloat16)
        down = jnp.dot(coarse, transfer[leaf], preferred_element_type=jnp.float32)
        combined = (far[leaf] + down).astype(jnp.bfloat16)
        out[:, leaf * size : (leaf + 1) * size] = near[leaf] + jnp.dot(
            combined, basis[leaf], preferred_element_type=jnp.float32
        )


def per_device(
    coords,
    charges,
    leaf_basis,
    transfer,
    leaf_skeleton,
    parent_skeleton,
    near_ids,
    near_mask,
    far_ids,
    far_mask,
    coarse_ids,
    coarse_mask,
):
    leaves_dev, rank, leaf_size = leaf_basis.shape
    systems = charges.shape[0]
    parents_dev = leaves_dev // CH
    subs = lax.axis_size("sub")
    groups = lax.axis_size("group")
    group_leaves = leaves_dev * subs
    first_leaf = lax.axis_index(("group", "sub")) * leaves_dev
    group_first = lax.axis_index("group") * group_leaves
    smem = pl.BlockSpec(memory_space=pltpu.SMEM)
    vmem = pl.BlockSpec(memory_space=pltpu.VMEM)
    pairs = leaves_dev * rank // 128
    parent_pairs = parents_dev * rank // 128
    bf16, f32, i32 = jnp.bfloat16, jnp.float32, jnp.int32
    shape = jax.ShapeDtypeStruct

    def params(mib):
        return pltpu.CompilerParams(vmem_limit_bytes=mib * 2**20)

    stride = pairs + groups * parent_pairs
    points = leaves_dev * leaf_size
    near_sources, joined, near_targets, leaf_targets, parent_targets = pl.pallas_call(
        functools.partial(prepare_kernel, subs, groups),
        out_shape=[
            shape((3 * leaves_dev, 32, 128), bf16),
            shape((stride, 32, 128), bf16),
            shape((leaves_dev, leaf_size, 16), bf16),
            shape((leaves_dev, rank, 16), bf16),
            shape((parents_dev, rank, 16), bf16),
        ],
        in_specs=[pl.BlockSpec(memory_space=pl.ANY)] * 6,
        out_specs=[vmem] * 5,
        scratch_shapes=[
            pltpu.VMEM((3, 3, points), f32),
            pltpu.VMEM((3, systems, points), bf16),
            pltpu.VMEM(leaf_basis.shape, bf16),
            pltpu.VMEM(transfer.shape, bf16),
            pltpu.VMEM(leaf_skeleton.shape, f32),
            pltpu.VMEM(parent_skeleton.shape, f32),
            pltpu.VMEM((16, points), f32),
            pltpu.VMEM((16, points), f32),
            pltpu.VMEM((systems, leaves_dev * rank), f32),
            pltpu.VMEM((systems, parents_dev * rank), f32),
            pltpu.SemaphoreType.DMA((6,)),
            pltpu.SemaphoreType.DMA((4,)),
            pltpu.SemaphoreType.DMA((4,)),
            pltpu.SemaphoreType.DMA((groups - 1,)),
            pltpu.SemaphoreType.DMA((groups - 1,)),
        ],
        compiler_params=pltpu.CompilerParams(
            vmem_limit_bytes=40 * 2**20, collective_id=0, has_side_effects=True
        ),
        name="prepare",
    )(coords, charges, leaf_basis, transfer, leaf_skeleton, parent_skeleton)
    group_packed = lax.all_gather(joined, "sub", axis=0, tiled=True)

    everyone = groups * subs * parents_dev
    ahead = lax.rem(
        coarse_ids - lax.axis_index("group") * (subs * parents_dev) + everyone, everyone
    )
    inside = lax.rem(ahead, subs * parents_dev)
    coarse_at = (
        (inside // parents_dev) * (groups * parents_dev)
        + (ahead // (subs * parents_dev)) * parents_dev
        + lax.rem(inside, parents_dev)
    )

    def item_rows(rows, slots, per_item):
        return -(-(rows * -(-slots // per_item) + 16) // 128)

    list_shapes = []
    for ids, per_item in ((near_ids, NEAR_SLOTS), (far_ids, FAR_SLOTS), (coarse_ids, FAR_SLOTS)):
        list_shapes.append(shape((ids.shape[0], 128), i32))
        list_shapes.append(shape((item_rows(*ids.shape, per_item), 128), i32))
    near_words, near_items, far_words, far_items, coarse_words, coarse_items = pl.pallas_call(
        lists_kernel,
        out_shape=list_shapes,
        in_specs=[vmem] * 6,
        out_specs=[vmem] * 6,
        compiler_params=params(40),
        name="lists",
    )(
        near_ids - (first_leaf - leaves_dev),
        near_mask,
        far_ids - group_first,
        far_mask,
        coarse_at,
        coarse_mask,
    )

    cost = pl.CostEstimate(flops=20_000_000_000, bytes_accessed=4_000_000, transcendentals=20_000_000)
    ln2 = 1.0 / LOG2E
    near = pl.pallas_call(
        functools.partial(near_kernel, ln2 / math.sqrt(near_ids.shape[1])),
        out_shape=shape((leaves_dev, systems, leaf_size), f32),
        in_specs=[smem] * 2 + [vmem] * 2,
        out_specs=vmem,
        cost_estimate=cost,
        compiler_params=params(40),
        name="near",
    )(near_words, near_items, near_targets, near_sources)

    return pl.pallas_call(
        functools.partial(
            far_kernel,
            ln2 / math.sqrt(far_ids.shape[1]),
            ln2 / math.sqrt(coarse_ids.shape[1]),
            pairs,
            stride,
        ),
        out_shape=shape((systems, leaves_dev * leaf_size), f32),
        in_specs=[smem] * 4 + [vmem] * 6,
        out_specs=vmem,
        scratch_shapes=[
            pltpu.VMEM((group_leaves, 32, 128), bf16),
            pltpu.VMEM((everyone, 32, 128), bf16),
            pltpu.VMEM((leaves_dev, systems, rank), f32),
            pltpu.VMEM((parents_dev, systems, rank), f32),
        ],
        compiler_params=params(56),
        name="far",
    )(
        far_words,
        far_items,
        coarse_words,
        coarse_items,
        leaf_targets,
        parent_targets,
        group_packed,
        transfer,
        leaf_basis,
        near,
    )


def solution(mesh):
    placed = (
        P(None, ("group", "sub")),
        P(None, ("group", "sub")),
        P(("group", "sub"), None, None),
        P(("group", "sub"), None, None),
        P(None, ("group", "sub")),
        P(None, ("group", "sub")),
        P(("group", "sub"), None),
        P(("group", "sub"), None),
        P(("group", "sub"), None),
        P(("group", "sub"), None),
        P(("group", "sub"), None),
        P(("group", "sub"), None),
    )
    return jax.shard_map(
        per_device, mesh=mesh, in_specs=placed, out_specs=P(None, ("group", "sub")), check_vma=False
    )
```

```python
import functools
import math

import jax
import jax.numpy as jnp
from jax import lax
from jax.experimental import pallas as pl
from jax.experimental.pallas import tpu as pltpu
from jax.sharding import PartitionSpec as P

CH = 8
NEAR_UNROLL, NEAR_SLOTS = 16, 2
FAR_UNROLL, FAR_SLOTS = 16, 4
ZEROS_AT, ITEMS_AT = 100, 127
LOG2E = 1.4426950408889634
STRETCH = math.sqrt(3.0) / 0.25 * LOG2E


def split_points(points):
    def top(x):
        return x.astype(jnp.bfloat16).astype(jnp.float32)

    scaled = (points - 0.5) * STRETCH
    high = top(scaled)
    low = top(scaled - high)
    whole = high + low
    squares = whole * whole
    norm = squares[0:1] + squares[1:2] + squares[2:3]
    n1 = top(norm)
    n2 = top(norm - n1)
    return high, low, (n1, n2, norm - n1 - n2)


def fill_rows(points, sources, targets):
    high, low, norm = split_points(points)
    sources[...] = jnp.ones_like(sources)
    targets[...] = jnp.ones_like(targets)
    sources[0:3, :] = high
    sources[3:6, :] = high
    sources[6:9, :] = low
    targets[0:3, :] = -2.0 * high
    targets[3:6, :] = -2.0 * low
    targets[6:9, :] = -2.0 * high
    for i, piece in enumerate(norm):
        sources[12 + i : 13 + i, :] = piece
        targets[9 + i : 10 + i, :] = piece
    sources[15:16, :] = jnp.zeros_like(norm[0])


def prepare_kernel(
    subs,
    groups,
    coords_in,
    charges_in,
    basis_in,
    transfer_in,
    leaf_skeleton_in,
    parent_skeleton_in,
    near_out,
    joined,
    near_targets,
    leaf_targets,
    parent_targets,
    points,
    values,
    basis,
    transfer,
    leaf_skeleton,
    parent_skeleton,
    rows_s,
    rows_t,
    coefs,
    parent_coefs,
    loads,
    halo_send,
    halo_recv,
    send,
    recv,
):
    leaves, rank, size = basis.shape
    pairs = leaves * rank // 128
    width = pairs // CH
    sub, group = lax.axis_index("sub"), lax.axis_index("group")
    right, left = lax.rem(sub + 1, subs), lax.rem(sub + subs - 1, subs)
    mesh_id = pl.DeviceIdType.MESH
    sides = [(group, right), (group, left)]
    partners = [(lax.rem(group + groups - d, groups), sub) for d in range(1, groups)]
    barrier = pltpu.get_barrier_semaphore()
    for partner in sides + partners:
        pl.semaphore_signal(barrier, inc=1, device_id=partner, device_id_type=mesh_id)
    moves = [
        (charges_in, values.at[0]),
        (basis_in, basis),
        (transfer_in, transfer),
        (parent_skeleton_in, parent_skeleton),
        (leaf_skeleton_in, leaf_skeleton),
        (coords_in, points.at[0]),
    ]
    held = [pltpu.make_async_copy(a, b, loads.at[i]) for i, (a, b) in enumerate(moves)]
    for copy in held:
        copy.start()
    pl.semaphore_wait(barrier, len(sides) + len(partners))
    halo = []
    for k, side in enumerate(sides):
        for n, (source, landing) in enumerate(((coords_in, points), (charges_in, values))):
            halo.append(
                pltpu.make_async_remote_copy(
                    src_ref=source,
                    dst_ref=landing.at[1 + k],
                    send_sem=halo_send.at[2 * k + n],
                    recv_sem=halo_recv.at[2 * k + n],
                    device_id=side,
                    device_id_type=mesh_id,
                )
            )
            halo[-1].start()

    def columns(out, width):
        for i in range(out.shape[0]):
            out[i] = rows_t[:, i * width : (i + 1) * width].T.astype(jnp.bfloat16)

    def block(rows, i):
        return rows[:, i * 128 : (i + 1) * 128].astype(jnp.bfloat16)

    for copy in held[:3]:
        copy.wait()
    for leaf in range(leaves):
        mine = lax.dot_general(
            values[0, :, leaf * size : (leaf + 1) * size],
            basis[leaf],
            (((1,), (1,)), ((), ())),
            preferred_element_type=jnp.float32,
        )
        coefs[:, leaf * rank : (leaf + 1) * rank] = mine
    for parent in range(leaves // CH):
        total = jnp.zeros((coefs.shape[0], rank), jnp.float32)
        for leaf in range(parent * CH, (parent + 1) * CH):
            total += lax.dot_general(
                coefs[:, leaf * rank : (leaf + 1) * rank].astype(jnp.bfloat16),
                transfer[leaf],
                (((1,), (1,)), ((), ())),
                preferred_element_type=jnp.float32,
            )
        parent_coefs[:, parent * rank : (parent + 1) * rank] = total

    def far_blocks(skeleton, numbers, first, count, targets):
        lanes = skeleton.shape[1]
        fill_rows(skeleton[...], rows_s.at[:, :lanes], rows_t.at[:, :lanes])
        for i in range(count):
            joined[first + i, :16, :] = block(rows_s, i)
            joined[first + i, 16:, :] = block(numbers, i)
        columns(targets, rank)

    held[3].wait()
    far_blocks(parent_skeleton, parent_coefs, pairs, width, parent_targets)
    across = []
    for k, partner in enumerate(partners):
        across.append(
            pltpu.make_async_remote_copy(
                src_ref=joined.at[pl.ds(pairs, width)],
                dst_ref=joined.at[pl.ds(pairs + (k + 1) * width, width)],
                send_sem=send.at[k],
                recv_sem=recv.at[k],
                device_id=partner,
                device_id_type=mesh_id,
            )
        )
        across[-1].start()
    held[4].wait()
    far_blocks(leaf_skeleton, coefs, 0, pairs, leaf_targets)

    def near_blocks(part, first):
        fill_rows(points[part], rows_s, rows_t)
        for leaf in range(leaves):
            near_out[first + leaf, :16, :] = block(rows_s, leaf)
            near_out[first + leaf, 16:, :] = values[part, :, leaf * size : (leaf + 1) * size]

    held[5].wait()
    near_blocks(0, leaves)
    columns(near_targets, size)
    for copy in halo[:2]:
        copy.wait()
    near_blocks(1, 0)
    for copy in halo[2:]:
        copy.wait()
    near_blocks(2, 2 * leaves)
    for copy in across:
        copy.wait()


def compact(ids, mask, per_item, words, items):
    rows, slots = ids.shape
    lane = lax.broadcasted_iota(jnp.int32, (rows, slots), 1)
    valid = mask != 0
    named = jnp.where(valid, ids, -1)
    count = jnp.zeros_like(ids)
    repeated = jnp.zeros_like(ids)
    for m in range(slots):
        same = jnp.where(ids == named[:, m : m + 1], 1, 0)
        count += same
        repeated += jnp.where(lane > m, same, 0)
    first = jnp.where(valid & (repeated == 0), 1, 0)
    ahead = jnp.where(
        lax.broadcasted_iota(jnp.int32, (slots, slots), 0)
        < lax.broadcasted_iota(jnp.int32, (slots, slots), 1),
        1.0,
        0.0,
    ).astype(jnp.bfloat16)
    place = jnp.dot(
        first.astype(jnp.float32).astype(jnp.bfloat16), ahead, preferred_element_type=jnp.float32
    ).astype(jnp.int32)
    packed = (ids * 128 + count) * first
    wide = lax.broadcasted_iota(jnp.int32, (rows, 128), 1)
    out = jnp.zeros((rows, 128), jnp.int32)
    for m in range(slots):
        out += jnp.where(wide == place[:, m : m + 1], packed[:, m : m + 1], 0)
    length = jnp.sum(first.astype(jnp.float32), axis=1, keepdims=True).astype(jnp.int32)
    blocks = jnp.broadcast_to((length + per_item - 1) // per_item, (rows, 128))
    until = jnp.where(
        lax.broadcasted_iota(jnp.int32, (rows, rows), 1)
        <= lax.broadcasted_iota(jnp.int32, (rows, rows), 0),
        1.0,
        0.0,
    )
    ends = jnp.dot(until, blocks.astype(jnp.float32), preferred_element_type=jnp.float32).astype(
        jnp.int32
    )
    starts = ends - blocks
    total = jnp.max(ends, axis=0, keepdims=True)
    words[...] = jnp.where(wide == ITEMS_AT, jnp.broadcast_to(total, (rows, 128)), out)
    for c in range(items.shape[0]):
        item = wide + c * 128
        owner = jnp.sum(jnp.where(item >= ends, 1, 0), axis=0, keepdims=True)
        start = jnp.max(jnp.where(item >= starts, starts, 0), axis=0, keepdims=True)
        entry = owner * 128 + (item[:1] - start) * per_item
        items[c : c + 1, :] = jnp.where(item[:1] < total, entry, (rows - 1) * 128 + ZEROS_AT)


def lists_kernel(near_ids, near_mask, far_ids, far_mask, coarse_ids, coarse_mask, *outs):
    compact(near_ids[...], near_mask[...], NEAR_SLOTS, outs[0], outs[1])
    compact(far_ids[...], far_mask[...], FAR_SLOTS, outs[2], outs[3])
    compact(coarse_ids[...], coarse_mask[...], FAR_SLOTS, outs[4], outs[5])


def tile_values(squared):
    squared = jnp.maximum(squared, 1e-12)
    u = squared * lax.rsqrt(squared)
    return ((u + LOG2E) * jnp.exp2(-u)).astype(jnp.bfloat16)


def add_items(words, items, per_item, unroll, targets, fetch, total, factor):
    def entry(row, lane):
        word = words[row, lane]
        count = jnp.bitwise_and(word, 127).astype(jnp.float32).astype(jnp.bfloat16)
        return lax.shift_right_logical(word, 7), count

    def step(i, carry):
        for k in range(unroll):
            item = i * unroll + k
            at = items[lax.shift_right_logical(item, 7), jnp.bitwise_and(item, 127)]
            row, lane = lax.shift_right_logical(at, 7), jnp.bitwise_and(at, 127)
            points, mine = fetch([entry(row, lane + s) for s in range(per_item)])
            squared = jnp.dot(targets[row], points, preferred_element_type=jnp.float32)
            total[row] += factor * lax.dot_general(
                mine,
                tile_values(squared),
                (((1,), (1,)), ((), ())),
                preferred_element_type=jnp.float32,
            )
        return carry

    total[...] = jnp.zeros_like(total)
    lax.fori_loop(0, (words[0, ITEMS_AT] + unroll - 1) // unroll, step, 0)


def near_kernel(factor, words, items, targets, held, out):
    def fetch(entries):
        points = [held[i, :16, :] for i, _ in entries]
        values = [held[i, 16:, :] * c for i, c in entries]
        return jnp.concatenate(points, axis=1), jnp.concatenate(values, axis=1)

    add_items(words, items, NEAR_SLOTS, NEAR_UNROLL, targets, fetch, out, factor)


def fetch_halves(spread):
    left = lax.broadcasted_iota(jnp.int32, (16, 128), 1) < 64

    def fetch(entries):
        points, values = [], []
        for (ia, ca), (ib, cb) in zip(entries[::2], entries[1::2]):
            points.append(jnp.where(left, spread[ia, :16, :], spread[ib, :16, :]))
            values.append(jnp.where(left, spread[ia, 16:, :] * ca, spread[ib, 16:, :] * cb))
        return jnp.concatenate(points, axis=1), jnp.concatenate(values, axis=1)

    return fetch


def spread_halves(packed, spread, offset, blocks, stride):
    left = lax.broadcasted_iota(jnp.int32, packed.shape[1:], 1) < 64

    def one(g, carry):
        for i in range(blocks):
            both = packed[g * stride + offset + i].astype(jnp.float32)
            turned = pltpu.roll(both, 64, 1)
            at = 2 * (g * blocks + i)
            spread[at] = jnp.where(left, both, turned).astype(jnp.bfloat16)
            spread[at + 1] = jnp.where(left, turned, both).astype(jnp.bfloat16)
        return carry

    lax.fori_loop(0, packed.shape[0] // stride, one, 0)


def far_kernel(
    far_factor,
    coarse_factor,
    pairs,
    stride,
    far_words,
    far_items,
    coarse_words,
    coarse_items,
    leaf_targets,
    parent_targets,
    packed,
    transfer,
    basis,
    near,
    out,
    leaf_spread,
    parent_spread,
    far,
    total,
):
    spread_halves(packed, parent_spread, pairs, stride - pairs, stride)
    spread_halves(packed, leaf_spread, 0, pairs, stride)
    add_items(
        coarse_words,
        coarse_items,
        FAR_SLOTS,
        FAR_UNROLL,
        parent_targets,
        fetch_halves(parent_spread),
        total,
        coarse_factor,
    )
    add_items(
        far_words,
        far_items,
        FAR_SLOTS,
        FAR_UNROLL,
        leaf_targets,
        fetch_halves(leaf_spread),
        far,
        far_factor,
    )
    leaves, _, size = basis.shape
    for leaf in range(leaves):
        coarse = total[leaf // CH].astype(jnp.bfloat16)
        down = jnp.dot(coarse, transfer[leaf], preferred_element_type=jnp.float32)
        combined = (far[leaf] + down).astype(jnp.bfloat16)
        out[:, leaf * size : (leaf + 1) * size] = near[leaf] + jnp.dot(
            combined, basis[leaf], preferred_element_type=jnp.float32
        )


def per_device(
    coords,
    charges,
    leaf_basis,
    transfer,
    leaf_skeleton,
    parent_skeleton,
    near_ids,
    near_mask,
    far_ids,
    far_mask,
    coarse_ids,
    coarse_mask,
):
    leaves_dev, rank, leaf_size = leaf_basis.shape
    systems = charges.shape[0]
    parents_dev = leaves_dev // CH
    subs = lax.axis_size("sub")
    groups = lax.axis_size("group")
    group_leaves = leaves_dev * subs
    first_leaf = lax.axis_index(("group", "sub")) * leaves_dev
    group_first = lax.axis_index("group") * group_leaves
    smem = pl.BlockSpec(memory_space=pltpu.SMEM)
    vmem = pl.BlockSpec(memory_space=pltpu.VMEM)
    pairs = leaves_dev * rank // 128
    parent_pairs = parents_dev * rank // 128
    bf16, f32, i32 = jnp.bfloat16, jnp.float32, jnp.int32
    shape = jax.ShapeDtypeStruct

    def params(mib):
        return pltpu.CompilerParams(vmem_limit_bytes=mib * 2**20)

    stride = pairs + groups * parent_pairs
    points = leaves_dev * leaf_size
    near_sources, joined, near_targets, leaf_targets, parent_targets = pl.pallas_call(
        functools.partial(prepare_kernel, subs, groups),
        out_shape=[
            shape((3 * leaves_dev, 32, 128), bf16),
            shape((stride, 32, 128), bf16),
            shape((leaves_dev, leaf_size, 16), bf16),
            shape((leaves_dev, rank, 16), bf16),
            shape((parents_dev, rank, 16), bf16),
        ],
        in_specs=[pl.BlockSpec(memory_space=pl.ANY)] * 6,
        out_specs=[vmem] * 5,
        scratch_shapes=[
            pltpu.VMEM((3, 3, points), f32),
            pltpu.VMEM((3, systems, points), bf16),
            pltpu.VMEM(leaf_basis.shape, bf16),
            pltpu.VMEM(transfer.shape, bf16),
            pltpu.VMEM(leaf_skeleton.shape, f32),
            pltpu.VMEM(parent_skeleton.shape, f32),
            pltpu.VMEM((16, points), f32),
            pltpu.VMEM((16, points), f32),
            pltpu.VMEM((systems, leaves_dev * rank), f32),
            pltpu.VMEM((systems, parents_dev * rank), f32),
            pltpu.SemaphoreType.DMA((6,)),
            pltpu.SemaphoreType.DMA((4,)),
            pltpu.SemaphoreType.DMA((4,)),
            pltpu.SemaphoreType.DMA((groups - 1,)),
            pltpu.SemaphoreType.DMA((groups - 1,)),
        ],
        compiler_params=pltpu.CompilerParams(
            vmem_limit_bytes=56 * 2**20, collective_id=0, has_side_effects=True
        ),
        name="prepare",
    )(coords, charges, leaf_basis, transfer, leaf_skeleton, parent_skeleton)
    group_packed = lax.all_gather(joined, "sub", axis=0, tiled=True)

    everyone = groups * subs * parents_dev
    ahead = lax.rem(
        coarse_ids - lax.axis_index("group") * (subs * parents_dev) + everyone, everyone
    )
    inside = lax.rem(ahead, subs * parents_dev)
    coarse_at = (
        (inside // parents_dev) * (groups * parents_dev)
        + (ahead // (subs * parents_dev)) * parents_dev
        + lax.rem(inside, parents_dev)
    )

    def item_rows(rows, slots, per_item):
        return -(-(rows * -(-slots // per_item) + 16) // 128)

    list_shapes = []
    for ids, per_item in ((near_ids, NEAR_SLOTS), (far_ids, FAR_SLOTS), (coarse_ids, FAR_SLOTS)):
        list_shapes.append(shape((ids.shape[0], 128), i32))
        list_shapes.append(shape((item_rows(*ids.shape, per_item), 128), i32))
    near_words, near_items, far_words, far_items, coarse_words, coarse_items = pl.pallas_call(
        lists_kernel,
        out_shape=list_shapes,
        in_specs=[vmem] * 6,
        out_specs=[vmem] * 6,
        compiler_params=params(40),
        name="lists",
    )(
        near_ids - (first_leaf - leaves_dev),
        near_mask,
        far_ids - group_first,
        far_mask,
        coarse_at,
        coarse_mask,
    )

    cost = pl.CostEstimate(flops=20_000_000_000, bytes_accessed=4_000_000, transcendentals=20_000_000)
    ln2 = 1.0 / LOG2E
    near = pl.pallas_call(
        functools.partial(near_kernel, ln2 / math.sqrt(near_ids.shape[1])),
        out_shape=shape((leaves_dev, systems, leaf_size), f32),
        in_specs=[smem] * 2 + [vmem] * 2,
        out_specs=vmem,
        cost_estimate=cost,
        compiler_params=params(40),
        name="near",
    )(near_words, near_items, near_targets, near_sources)

    return pl.pallas_call(
        functools.partial(
            far_kernel,
            ln2 / math.sqrt(far_ids.shape[1]),
            ln2 / math.sqrt(coarse_ids.shape[1]),
            pairs,
            stride,
        ),
        out_shape=shape((systems, leaves_dev * leaf_size), f32),
        in_specs=[smem] * 4 + [vmem] * 6,
        out_specs=vmem,
        scratch_shapes=[
            pltpu.VMEM((group_leaves, 32, 128), bf16),
            pltpu.VMEM((everyone, 32, 128), bf16),
            pltpu.VMEM((leaves_dev, systems, rank), f32),
            pltpu.VMEM((parents_dev, systems, rank), f32),
        ],
        compiler_params=params(56),
        name="far",
    )(
        far_words,
        far_items,
        coarse_words,
        coarse_items,
        leaf_targets,
        parent_targets,
        group_packed,
        transfer,
        leaf_basis,
        near,
    )


def solution(mesh):
    placed = (
        P(None, ("group", "sub")),
        P(None, ("group", "sub")),
        P(("group", "sub"), None, None),
        P(("group", "sub"), None, None),
        P(None, ("group", "sub")),
        P(None, ("group", "sub")),
        P(("group", "sub"), None),
        P(("group", "sub"), None),
        P(("group", "sub"), None),
        P(("group", "sub"), None),
        P(("group", "sub"), None),
        P(("group", "sub"), None),
    )
    return jax.shard_map(
        per_device, mesh=mesh, in_specs=placed, out_specs=P(None, ("group", "sub")), check_vma=False
    )
```
